32 devices in a mesh: groups: 1, expert: 32 (over z, y, x, core).
Axes of the slice: x: 2, y: 2, z: 4, core: 2. Of those that a mesh axis runs over, the one named last changes fastest.
Arguments:
- hidden: bfloat16 [384, 4096], P(('groups', 'expert')), may hold values from -6 to 6
- expert_ids: int32 [384, 8], P(('groups', 'expert')), may hold values from 0 to 15, all different within a row; in each aligned block of 12 rows (0 to 11, 12 to 23, ...) at most 9 rows name the same one
- gate_raw: float32 [384, 8], P(('groups', 'expert')), may hold values from 0.05 to 1
- w_gate: bfloat16 [32, 4096, 384], P('expert'), may hold values from -0.09375 to 0.09375
- w_up: bfloat16 [32, 4096, 384], P('expert'), may hold values from -0.09375 to 0.09375
- w_down: bfloat16 [32, 384, 4096], P('expert'), may hold values from -0.21875 to 0.21875
Outputs:
- moe_out: bfloat16 [384, 4096], P(('groups', 'expert'))
The draws below stay inside these ranges and needn't reach their ends.
Inputs may be any that keep to these rules, and one draw needn't show every extreme that they name: `expert_ids`: each row names 8 different experts. Among the 12 rows of one device (aligned blocks) no expert is named by more than 9 rows, a bound that some block reaches of some device in every draw.
All inputs are finite; a program needn't handle non-finite values.
Results may differ from the reference program's by a relative error of at most 0.0085.
Values may be sent and summed in bfloat16 or wider, within the bound.
No kernel may reach another device: no remote copies, remote signals or barrier semaphores. Data moves between devices by JAX's collectives and lax.ppermute only.
A program may use at most 128 MiB of HBM per device.

```python
import math
import jax
import jax.numpy as jnp
import numpy as np
from jax import lax

D = 4096
FF = 768
TOP = 8
ROWS_DEV = 12
EXPERTS = 16
CAP = 9
ROWS = 384
N_EXPERT = 32


def steps_of(rng, extent, split, low, largest):
    def one(position, blocks):
        steps = jax.random.uniform(jax.random.fold_in(jax.random.fold_in(rng, 6), position), (blocks,), jnp.float32, low / len(split), largest / len(split))
        return jnp.repeat(jnp.exp(steps), extent[position] // blocks).reshape((-1,) + (1,) * (len(extent) - position - 1))

    loudness = one(*split[0])
    for cut in split[1:]:
        loudness = loudness * one(*cut)
    return loudness


def shared_out(rng, own, number, rows, number_of, top, most, slope):
    sequence = jax.random.permutation(rng, number_of)
    crowded, ordinary = load_shares(number_of, rows * top, most, slope, True), load_shares(number_of, rows * top, most, slope, False)
    places = jnp.arange(number_of)

    def named(tallies, turn):
        used = int((tallies > 0).sum())
        fixed = max(1, used // 4)
        moved = fixed + (places - fixed + turn * (used - fixed)) % max(1, number_of - fixed)
        return jnp.zeros((number_of,), jnp.int32).at[sequence[jnp.where(places < fixed, places, moved)]].set(jnp.asarray(tallies, jnp.int32))

    tallies = jnp.where(number % 4 == 0, named(crowded, number // 4), named(ordinary, number - number // 4 - 1))
    mixed = jax.random.permutation(jax.random.fold_in(own, 3), number_of)
    giver, sink = mixed[0:number_of // 2 * 2:2], mixed[1:number_of // 2 * 2:2]
    margin = jnp.minimum(tallies[giver] - 1, most - tallies[sink]) // 2
    margin = jnp.where((giver == sequence[0]) | (sink == sequence[0]) | (tallies[sink] == 0), 0, jnp.maximum(margin, 0))
    moved = jax.random.randint(jax.random.fold_in(own, 4), (number_of // 2,), 0, 1 << 20) % (margin + 1)
    tallies = tallies.at[giver].add(-moved).at[sink].add(moved)
    items = jnp.searchsorted(jnp.cumsum(tallies), jnp.arange(rows * top), side="right").astype(jnp.int32)
    grid = items.reshape(top, rows).T
    grid = grid[jax.random.permutation(jax.random.fold_in(own, 1), rows)]
    turn = jax.random.randint(jax.random.fold_in(own, 2), (rows, 1), 0, top)
    return jnp.take_along_axis(grid, (jnp.arange(top)[None, :] + turn) % top, axis=1)


def load_shares(number_of, total, limit, skew, full):
    portions = [(1 << 20) // math.isqrt(grade ** skew) + 1 for grade in range(1, number_of + 1)]
    largest = limit if full else min(limit, max(-(-total // number_of), total * portions[0] // sum(portions)))
    least = 1 if total - largest >= number_of - 1 else 0
    counts, surplus = [largest] + [least] * (number_of - 1), total - largest - least * (number_of - 1)
    while surplus > 0:
        candidates = [i for i in range(1, number_of) if counts[i] < largest] or [i for i in range(1, number_of) if counts[i] < limit]
        whole, budget = sum([portions[i] for i in candidates]), surplus
        for i in candidates:
            extra = min(limit - counts[i], max(1, budget * portions[i] // whole), surplus)
            counts[i] = counts[i] + extra
            surplus = surplus - extra
    return np.array(counts)


def centred(stream_key, extent, scale, reach, cuts=(), dtype=jnp.bfloat16):
    entries = scale * jax.random.normal(stream_key, extent, jnp.float32)
    if cuts:
        entries = entries * steps_of(stream_key, extent, cuts, -0.22, 0.18)
    return jnp.clip(entries, -reach, reach).astype(dtype)


def setup_inputs(seed: int = 0, part: int = 0) -> dict:
    streams_of = jax.random.split(jax.random.key(seed), 7)
    part_keys = jax.random.split(jax.random.fold_in(streams_of[6], part), 7)
    hidden = centred(part_keys[0], (ROWS, D), 1.0, 6.0, ((0, 32),))
    expert_ids_keys = jax.random.split(jax.random.fold_in(part_keys[1], 1), ROWS // ROWS_DEV)
    expert_ids_turns = jax.random.permutation(jax.random.fold_in(part_keys[1], 3), ROWS // ROWS_DEV)
    expert_ids = jax.vmap(lambda own, number: shared_out(jax.random.fold_in(part_keys[1], 2), own, number, ROWS_DEV, EXPERTS, TOP, CAP, 2))(expert_ids_keys, expert_ids_turns).reshape((ROWS, TOP))
    gate_raw = jnp.clip(jnp.exp(math.log(1.0) - 2.9957323 * jax.random.uniform(part_keys[2], (ROWS, TOP), jnp.float32) ** steps_of(part_keys[2], (ROWS, TOP), ((0, 32),), -0.2, 0.2)), 0.05, 1.0)
    w_gate = centred(streams_of[3], (2 * EXPERTS, D, FF // 2), D ** -0.5, 0.09375, ((0, 32),))
    w_up = centred(streams_of[4], (2 * EXPERTS, D, FF // 2), D ** -0.5, 0.09375, ((0, 32),))
    w_down = centred(streams_of[5], (2 * EXPERTS, FF // 2, D), FF ** -0.5, 0.21875, ((0, 32),))
    return dict(hidden=hidden, expert_ids=expert_ids, gate_raw=gate_raw, w_gate=w_gate, w_up=w_up, w_down=w_down)


def reference(hidden, expert_ids, gate_raw, w_gate, w_up, w_down):
    weight = gate_raw / jnp.sum(gate_raw, axis=1, keepdims=True)
    listed = N_EXPERT * CAP
    width = hidden.shape[1]

    def one_expert(total, expert):
        hit = expert_ids == expert
        share = jnp.sum(jnp.where(hit, weight, 0.0), axis=1)
        used = jnp.any(hit, axis=1)
        order = jnp.argsort(jnp.where(used, 0, 1).astype(jnp.int32), stable=True)[:listed].astype(jnp.int32)
        picked = jnp.take(hidden, order, axis=0)
        result = jnp.zeros((listed, width), jnp.float32)
        for half in range(2):
            index = (2 * expert + half).astype(jnp.int32)
            gate_mat = lax.dynamic_index_in_dim(w_gate, index, 0, keepdims=False)
            up_mat = lax.dynamic_index_in_dim(w_up, index, 0, keepdims=False)
            down_mat = lax.dynamic_index_in_dim(w_down, index, 0, keepdims=False)
            gate = jnp.dot(picked, gate_mat, preferred_element_type=jnp.float32)
            upper = jnp.dot(picked, up_mat, preferred_element_type=jnp.float32)
            inner = (jax.nn.silu(gate) * upper).astype(jnp.bfloat16)
            part = jnp.dot(inner, down_mat, preferred_element_type=jnp.float32).astype(jnp.bfloat16)
            result = result + part.astype(jnp.float32)
        scale = jnp.take(jnp.where(used, share, 0.0), order, axis=0)
        total = total.at[order].add(scale[:, None] * result)
        return total, None

    start = jnp.zeros(hidden.shape, jnp.float32)
    total, unused = lax.scan(one_expert, start, jnp.arange(EXPERTS).astype(jnp.int32))
    return total.astype(jnp.bfloat16)
```

```python
import jax
import jax.numpy as jnp
from jax import lax
from jax.sharding import PartitionSpec as P

BF16 = jnp.bfloat16
F32 = jnp.float32
TILE = 8


def permute(value, devices, flip_of):
    pairs = [(device, device ^ flip_of(device)) for device in range(devices)]
    return lax.ppermute(value, "expert", pairs)


def first_flip(device):
    return 2 if device % 2 == 0 else 4


def second_flip(device):
    return 4 if device % 2 == 0 else 2


def fold(rows):
    half = rows.shape[1] // 2
    rest = rows[TILE:]
    return jnp.concatenate(
        [rows[:TILE], jnp.concatenate([rest[:, :half], rest[:, half:]], axis=0)], axis=1
    )


def unfold(block, width):
    half = width // 2
    part = TILE // 2
    rest = jnp.concatenate([block[:part, width:], block[part:, width:]], axis=1)
    return jnp.concatenate([block[:, :width], rest], axis=0)


def side_of(weight, expert_ids, experts):
    hit = expert_ids[:, :, None] == jnp.arange(experts)
    dense = jnp.sum(jnp.where(hit, weight[:, :, None], 0.0), axis=1)
    high = lax.reduce_precision(dense, 8, 7)
    low = dense - high
    return jnp.concatenate([high, low], axis=1).astype(BF16)


def expert_rows(blocks, width, experts, mine, weights):
    count = blocks.shape[0] // TILE
    part = TILE // 2
    half = width // 2
    main = blocks[:, :width]
    rest = blocks[:, width : width + half].reshape(count, 2, part, half)
    rest = rest.transpose(0, 2, 1, 3).reshape(count * part, width)
    flat = jnp.concatenate([main, rest], axis=0)
    side = blocks[:, width + half :].astype(F32)
    lane = jnp.arange(side.shape[1])
    pick = (lane == mine) | (lane == mine + experts)
    pick_rest = (lane == mine + 2 * experts) | (lane == mine + 3 * experts)
    scale = jnp.sum(jnp.where(pick, side, 0.0), axis=1)
    scale_rest = jnp.sum(jnp.where(pick_rest, side, 0.0), axis=1)
    scale_rest = scale_rest.reshape(count, TILE)[:, :part].reshape(count * part)
    scale = jnp.concatenate([scale, scale_rest])[:, None]
    total = 0.0
    for gate_mat, up_mat, down_mat in weights:
        gate = jnp.dot(flat, gate_mat, preferred_element_type=F32)
        upper = jnp.dot(flat, up_mat, preferred_element_type=F32)
        inner = (jax.nn.silu(gate) * upper * scale).astype(BF16)
        total = total + jnp.dot(inner, down_mat, preferred_element_type=F32)
    out = total.astype(BF16)
    rest = out[count * TILE :].reshape(count, part, 2, half).transpose(0, 2, 1, 3)
    return jnp.concatenate([out[: count * TILE], rest.reshape(count * TILE, half)], axis=1)


def add(a, b):
    return (a.astype(F32) + b.astype(F32)).astype(BF16)


def per_device(hidden, expert_ids, gate_raw, w_gate, w_up, w_down):
    devices = lax.axis_size("expert")
    experts = devices // 2
    levels = devices // 8
    rows, top = expert_ids.shape
    width = hidden.shape[1]
    mine = lax.axis_index("expert") // 2
    go = lambda value, flip: permute(value, devices, flip)

    weight = gate_raw / jnp.sum(gate_raw, axis=1, keepdims=True)
    side = side_of(weight, expert_ids, experts)
    spare = -(4 * experts) % 128
    side = jnp.concatenate(
        [side[:TILE], jnp.pad(side[TILE:], ((0, 2 * TILE - rows), (0, 0))), jnp.zeros((TILE, spare), BF16)],
        axis=1,
    )
    own = jnp.concatenate([fold(hidden), side], axis=1)

    level = [own] + [None] * (levels - 1)
    for step in reversed(range(1, levels)):
        level[step] = go(own, lambda device, s=step: 8 * s)
    weights = [(w_gate[0], w_up[0], w_down[0])]
    weights.append(tuple(go(w, lambda device: 1) for w in weights[0]))

    half = levels // 2
    results = []
    for group in (level[:half], level[half:]):
        here = jnp.concatenate(group, axis=0)
        pair = jnp.concatenate([here, go(here, first_flip)], axis=0)
        blocks = jnp.concatenate([pair, go(pair, second_flip)], axis=0)
        results.append(expert_rows(blocks, width, experts, mine, weights))

    sums = []
    for partial in reversed(results):
        count = partial.shape[0] // 2
        pair = add(partial[:count], go(partial[count:], second_flip))
        count = count // 2
        here = add(pair[:count], go(pair[count:], first_flip))
        sums.append(here.reshape(half, TILE, -1))
    far, near = sums
    total = near[0].astype(F32)
    for step in reversed(range(1, levels)):
        block = near[step] if step < half else far[step - half]
        total = total + go(block, lambda device, s=step: 8 * s).astype(F32)
    return unfold(total.astype(BF16), width)


def solution(mesh):
    placed = (
        P(("groups", "expert"), None),
        P(("groups", "expert"), None),
        P(("groups", "expert"), None),
        P("expert", None, None),
        P("expert", None, None),
        P("expert", None, None),
    )
    return jax.shard_map(
        per_device,
        mesh=mesh,
        in_specs=placed,
        out_specs=P(("groups", "expert"), None),
        check_vma=False,
    )
```

```python
import functools

import jax
import jax.numpy as jnp
from jax import lax
from jax.experimental import pallas as pl
from jax.experimental.pallas import tpu as pltpu
from jax.sharding import PartitionSpec as P

BF16 = jnp.bfloat16
F32 = jnp.float32
TILE = 8
STEP = 512
NSTEP = 512


def permute(value, devices, flip_of):
    pairs = [(device, device ^ flip_of(device)) for device in range(devices)]
    return lax.ppermute(value, "expert", pairs)


def first_flip(device):
    return 2 if device % 2 == 0 else 4


def second_flip(device):
    return 4 if device % 2 == 0 else 2


def fold(rows):
    half = rows.shape[1] // 2
    rest = rows[TILE:]
    return jnp.concatenate(
        [rows[:TILE], jnp.concatenate([rest[:, :half], rest[:, half:]], axis=0)], axis=1
    )


def unfold(block, width):
    half = width // 2
    part = TILE // 2
    rest = jnp.concatenate([block[:part, width:], block[part:, width:]], axis=1)
    return jnp.concatenate([block[:, :width], rest], axis=0)


def side_of(weight, expert_ids, experts):
    hit = expert_ids[:, :, None] == jnp.arange(experts)
    dense = jnp.sum(jnp.where(hit, weight[:, :, None], 0.0), axis=1)
    high = lax.reduce_precision(dense, 8, 7)
    low = dense - high
    return jnp.concatenate([high, low], axis=1).astype(BF16)


def swap_halves(value):
    rows, width = value.shape
    tiles = value.reshape(rows // TILE, TILE, width)
    return pltpu.roll(tiles, TILE // 2, 1).reshape(rows, width)


def expert_kernel(experts, width, mine, here, first, second, *refs):
    weights, (keep, send), inner = refs[:6], refs[6:8], refs[8]
    half = width // 2
    parts = (here, first, second)
    rows = sum(part.shape[0] for part in parts)
    upper = lax.broadcasted_iota(jnp.int32, (rows, 1), 0) % TILE < TILE // 2

    side = jnp.concatenate([part[:, width + half :] for part in parts], axis=0).astype(F32)
    lane = lax.broadcasted_iota(jnp.int32, side.shape, 1)
    turn = lane - mine[0]
    scale = jnp.sum(jnp.where((turn == 0) | (turn == experts), side, 0.0), axis=1, keepdims=True)
    turn = turn - 2 * experts
    scale_rest = jnp.sum(jnp.where((turn == 0) | (turn == experts), side, 0.0), axis=1, keepdims=True)

    def columns(start, size):
        return [part[:, start : start + size] for part in parts]

    def product(mat):
        low = high = None
        for start in range(0, half, STEP):
            rest = columns(width + start, STEP)
            a = jnp.concatenate(columns(start, STEP) + rest, axis=0)
            b = jnp.concatenate(columns(half + start, STEP) + rest, axis=0)
            u = jnp.dot(a, mat[start : start + STEP], preferred_element_type=F32)
            v = jnp.dot(b, mat[half + start : half + start + STEP], preferred_element_type=F32)
            low = u if low is None else low + u
            high = v if high is None else high + v
        rest = jnp.where(upper, low[rows:], high[rows:])
        return low[:rows] + high[:rows], rest + swap_halves(rest)

    hidden_units = weights[0].shape[1]
    for side_of_chip in range(2):
        gate, gate_rest = product(weights[3 * side_of_chip])
        up, up_rest = product(weights[3 * side_of_chip + 1])
        at = side_of_chip * hidden_units
        inner[:rows, at : at + hidden_units] = (jax.nn.silu(gate) * up * scale).astype(BF16)
        inner[rows:, at : at + hidden_units] = (jax.nn.silu(gate_rest) * up_rest * scale_rest).astype(BF16)

    def down(start):
        return sum(
            jnp.dot(
                inner[:, at * hidden_units : (at + 1) * hidden_units],
                weights[3 * at + 2][:, start : start + NSTEP],
                preferred_element_type=F32,
            )
            for at in range(2)
        )

    kept = keep.shape[0]
    for start in range(0, half, NSTEP):
        low, high = down(start), down(half + start)
        rest = jnp.where(upper, low[rows:], high[rows:])
        for value, at in ((low, start), (high, half + start), (rest, width + start)):
            value = value[:rows].astype(BF16)
            keep[:, at : at + NSTEP] = value[:kept]
            send[:, at : at + NSTEP] = value[kept:]


def expert_rows(parts, width, mine, experts, weights):
    rows = sum(part.shape[0] for part in parts)
    out = jax.ShapeDtypeStruct((rows // 2, width + width // 2), BF16)
    flat = [pltpu.with_memory_space_constraint(w, pltpu.VMEM) for half in weights for w in half]
    units = flat[0].shape[1]
    vmem = pl.BlockSpec(memory_space=pltpu.VMEM)
    return pl.pallas_call(
        functools.partial(expert_kernel, experts, width),
        out_shape=(out, out),
        in_specs=[pl.BlockSpec(memory_space=pltpu.SMEM)] + [vmem] * (3 + len(flat)),
        out_specs=(vmem, vmem),
        scratch_shapes=[pltpu.VMEM((2 * rows, 2 * units), BF16)],
        compiler_params=pltpu.CompilerParams(vmem_limit_bytes=24 << 20),
    )(mine, *parts, *flat)


def add(a, b):
    return (a.astype(F32) + b.astype(F32)).astype(BF16)


def per_device(hidden, expert_ids, gate_raw, w_gate, w_up, w_down):
    devices = lax.axis_size("expert")
    experts = devices // 2
    levels = devices // 8
    rows, top = expert_ids.shape
    width = hidden.shape[1]
    mine = (lax.axis_index("expert") // 2).reshape(1)
    go = lambda value, flip: permute(value, devices, flip)

    weight = gate_raw / jnp.sum(gate_raw, axis=1, keepdims=True)
    side = side_of(weight, expert_ids, experts)
    spare = -(4 * experts) % 128
    side = jnp.concatenate(
        [side[:TILE], jnp.concatenate([side[TILE:]] * 2, axis=0), jnp.zeros((TILE, spare), BF16)],
        axis=1,
    )
    own = jnp.concatenate([fold(hidden), side], axis=1)

    level = [own] + [None] * (levels - 1)
    for step in reversed(range(1, levels)):
        level[step] = go(own, lambda device, s=step: 8 * s)
    weights = [(w_gate[0], w_up[0], w_down[0])]
    weights.append(tuple(go(w, lambda device: 1) for w in weights[0]))

    half = levels // 2
    results = []
    for group in (level[:half], level[half:]):
        here = jnp.concatenate(group, axis=0)
        first = go(here, first_flip)
        second = go(jnp.concatenate([here, first], axis=0), second_flip)
        results.append(expert_rows((here, first, second), width, mine, experts, weights))

    sums = []
    for keep, send in reversed(results):
        pair = add(keep, go(send, second_flip))
        count = pair.shape[0] // 2
        here = add(pair[:count], go(pair[count:], first_flip))
        sums.append(here.reshape(half, TILE, -1))
    far, near = sums
    total = near[0].astype(F32)
    for step in reversed(range(1, levels)):
        block = near[step] if step < half else far[step - half]
        total = total + go(block, lambda device, s=step: 8 * s).astype(F32)
    return unfold(total.astype(BF16), width)


def solution(mesh):
    placed = (
        P(("groups", "expert"), None),
        P(("groups", "expert"), None),
        P(("groups", "expert"), None),
        P("expert", None, None),
        P("expert", None, None),
        P("expert", None, None),
    )
    return jax.shard_map(
        per_device,
        mesh=mesh,
        in_specs=placed,
        out_specs=P(("groups", "expert"), None),
        check_vma=False,
    )
```

```python
import functools

import jax
import jax.numpy as jnp
from jax import lax
from jax.experimental import pallas as pl
from jax.experimental.pallas import tpu as pltpu
from jax.sharding import PartitionSpec as P

BF16 = jnp.bfloat16
F32 = jnp.float32
TILE = 8
HALF_TILE = 4
LANES = 128
STEP = 512
PIECES = 4
COST = 4 << 20
VMEM = pl.BlockSpec(memory_space=pltpu.VMEM)
SMEM = pl.BlockSpec(memory_space=pltpu.SMEM)
HBM = pl.BlockSpec(memory_space=pltpu.HBM)


def call(kernel, out_shape, in_specs, args, scratch=(), limit=8, flops=0, moved=0):
    args = [
        pltpu.with_memory_space_constraint(arg, pltpu.HBM) if spec is HBM else arg
        for arg, spec in zip(args, in_specs)
    ]
    single = not isinstance(out_shape, tuple)
    return pl.pallas_call(
        kernel,
        out_shape=out_shape,
        in_specs=in_specs,
        out_specs=VMEM if single else (VMEM,) * len(out_shape),
        scratch_shapes=scratch,
        compiler_params=pltpu.CompilerParams(vmem_limit_bytes=limit << 20),
        cost_estimate=pl.CostEstimate(flops=flops, bytes_accessed=moved, transcendentals=0),
    )(*args)


def upper_rows(shape):
    return lax.broadcasted_iota(jnp.int32, shape, 0) < HALF_TILE


def swap(tile):
    return pltpu.roll(tile, HALF_TILE, 0)


def fold_kernel(experts, *refs):
    sources, out, (ids, gate, hidden, turned, sems) = refs[:3], refs[3], refs[4:]
    copies = [
        pltpu.make_async_copy(source, target, sems.at[i])
        for i, (source, target) in enumerate(zip(sources, (ids, gate, hidden)))
    ]
    for copy in copies:
        copy.start()
    copies[0].wait()
    copies[1].wait()
    rows, width = hidden.shape
    half = width // 2
    top = ids.shape[0]
    lanes = turned.shape[0]
    raw = gate[...]
    weight = raw / jnp.sum(raw, axis=0, keepdims=True)
    expert = lax.broadcasted_iota(jnp.int32, (lanes, rows), 0) % experts
    dense = jnp.zeros((lanes, rows), F32)
    for t in range(top):
        dense = jnp.where(ids[t : t + 1, :] == expert, weight[t : t + 1, :], dense)
    turned[:, :rows] = dense
    dense = turned[...].T
    high = dense.astype(BF16).astype(F32)
    first, last = high[:TILE], high[TILE : 2 * TILE]
    low_first, low_last = dense[:TILE] - first, dense[TILE : 2 * TILE] - last
    upper = upper_rows((TILE, lanes))
    last = jnp.where(upper, last, swap(last))
    low_last = jnp.where(upper, low_last, swap(low_last))
    role = lax.broadcasted_iota(jnp.int32, (TILE, lanes), 1) // experts
    side = jnp.where(
        role == 0,
        first,
        jnp.where(role == 1, low_first, jnp.where(role == 2, last, jnp.where(role == 3, low_last, 0.0))),
    )
    out[:, width + half :] = side.astype(BF16)
    copies[2].wait()
    out[:, :width] = hidden[:TILE, :]
    rest = hidden[TILE:, :].astype(F32)
    out[:, width : width + half] = jnp.concatenate([rest[:, :half], rest[:, half:]], axis=0).astype(BF16)


def fold_rows(hidden, expert_ids, gate_raw, experts):
    rows, width = hidden.shape
    lanes = -(-4 * experts // LANES) * LANES
    out = jax.ShapeDtypeStruct((TILE, width + width // 2 + lanes), BF16)
    return call(
        functools.partial(fold_kernel, experts),
        out,
        [HBM] * 3,
        (expert_ids.T, gate_raw.T, hidden),
        [
            pltpu.VMEM(expert_ids.T.shape, expert_ids.dtype),
            pltpu.VMEM(gate_raw.T.shape, F32),
            pltpu.VMEM(hidden.shape, BF16),
            pltpu.VMEM((lanes, LANES), F32),
            pltpu.SemaphoreType.DMA((3,)),
        ],
    )


def pair_kernel(experts, width, *refs):
    parts, out = refs[:-1], refs[-1]
    half = width // 2

    def tiles(start, size):
        values = [part[:, start : start + size].astype(F32) for part in parts]
        return [value[at : at + TILE] for value in values for at in range(0, value.shape[0], TILE)]

    lanes = out.shape[1] - width

    def put(at, size, firsts, lasts):
        rows = [row for a, b, last in zip(firsts[::2], firsts[1::2], lasts) for row in (a, b, last)]
        out[:, at : at + size] = jnp.concatenate(rows, axis=0).astype(BF16)

    upper = upper_rows((TILE, STEP))
    for start in range(0, half, STEP):
        rest = tiles(width + start, STEP)
        for at, turn in ((start, False), (half + start, True)):
            lasts = [
                jnp.where(upper, swap(a) if turn else a, b if turn else swap(b))
                for a, b in zip(rest[::2], rest[1::2])
            ]
            put(at, STEP, tiles(at, STEP), lasts)
    side = tiles(width + half, lanes)
    first = lax.broadcasted_iota(jnp.int32, (TILE, lanes), 1) < 2 * experts
    upper = upper_rows((TILE, lanes))
    put(
        width,
        lanes,
        [jnp.where(first, value, 0.0) for value in side],
        [jnp.where(first, 0.0, jnp.where(upper, a, b)) for a, b in zip(side[::2], side[1::2])],
    )


def pair_rows(parts, width, experts):
    lanes = parts[0].shape[1] - width - width // 2
    rows = sum(part.shape[0] for part in parts)
    out = jax.ShapeDtypeStruct((rows + rows // 2, width + lanes), BF16)
    return call(functools.partial(pair_kernel, experts, width), out, [VMEM] * len(parts), parts)


def split_kernel(order, *refs):
    parts, outs = refs[: -len(order)], refs[-len(order) :]
    rows, width = parts[0].shape
    half = width // 2
    upper = upper_rows((TILE, STEP))

    def tiles(at):
        total = sum(part[:, at : at + STEP].astype(F32)[:rows] for part in parts)
        return [total[row : row + TILE] for row in range(0, rows, TILE)]

    def put(at, values):
        for out, blocks in zip(outs, order):
            value = jnp.concatenate([values[block] for block in blocks], axis=0)
            out[:, at : at + STEP] = value.astype(BF16)

    for start in range(0, half, STEP):
        low, high = tiles(start), tiles(half + start)
        rest = []
        for a, b in zip(low[2::3], high[2::3]):
            rest += [jnp.where(upper, a, swap(b)), jnp.where(upper, swap(a), b)]
        put(start, [tile for i, tile in enumerate(low) if i % 3 < 2])
        put(half + start, [tile for i, tile in enumerate(high) if i % 3 < 2])
        put(width + start, rest)


def split_rows(parts, order, cost=0):
    width = parts[0].shape[1]
    shapes = tuple(jax.ShapeDtypeStruct((TILE * len(blocks), width + width // 2), BF16) for blocks in order)
    return call(functools.partial(split_kernel, order), shapes, [VMEM] * len(parts), parts, moved=cost)


def last_kernel(*refs):
    parts, out = refs[:-1], refs[-1]
    rows, width = out.shape
    half = width // 2
    for start in range(0, half, STEP):
        low, high, rest = (
            sum(part[:, at : at + STEP].astype(F32)[:TILE] for part in parts)
            for at in (start, half + start, width + start)
        )
        out[:, start : start + STEP] = jnp.concatenate([low, rest[:HALF_TILE]], axis=0).astype(BF16)
        out[:, half + start : half + start + STEP] = jnp.concatenate(
            [high, rest[HALF_TILE:]], axis=0
        ).astype(BF16)


def last_rows(parts, rows, width):
    return call(last_kernel, jax.ShapeDtypeStruct((rows, width), BF16), [VMEM] * len(parts), parts)


def fetch_kernel(*refs):
    count = len(refs) // 2
    sources, targets, sems = refs[:count], refs[count:-1], refs[-1]
    copies = []
    for i, (source, target) in enumerate(zip(sources, targets)):
        rows = source.shape[0] // PIECES
        for j in range(PIECES):
            at = pl.ds(j * rows, rows)
            copies.append(pltpu.make_async_copy(source.at[at], target.at[at], sems.at[i, j]))
    for copy in copies:
        copy.start()
    for copy in copies:
        copy.wait()


def fetch(arrays):
    return call(
        fetch_kernel,
        tuple(pltpu.VMEM(w.shape, w.dtype) for w in arrays),
        [HBM] * len(arrays),
        arrays,
        [pltpu.SemaphoreType.DMA((len(arrays), PIECES))],
    )


def expert_kernel(experts, count, mine, *refs):
    parts, own, others, source = refs[:count], refs[count : count + 3], refs[count + 3 : count + 5], refs[count + 5]
    outs, (xs, inner, last, sem) = refs[count + 6 : -4], refs[-4:]
    others += (last,)
    copy = pltpu.make_async_copy(source, last, sem)
    copy.start()
    width = outs[0].shape[1]
    units = own[0].shape[1]

    for start in range(0, width, STEP):
        xs[:, start : start + STEP] = jnp.concatenate(
            [part[:, start : start + STEP].astype(F32) for part in parts], axis=0
        ).astype(BF16)
    side = jnp.concatenate([part[:, width:].astype(F32) for part in parts], axis=0)
    lane = lax.broadcasted_iota(jnp.int32, side.shape, 1)
    scale = jnp.sum(jnp.where(lane % experts == mine[0], side, 0.0), axis=1, keepdims=True)

    for at, (gate, up, unused) in enumerate((own, others)):
        for tile in range(0, units, LANES):
            piece = slice(tile, tile + LANES)
            total = jnp.dot(
                xs[...],
                jnp.concatenate([gate[:, piece], up[:, piece]], axis=1),
                preferred_element_type=F32,
            )
            value = jax.nn.silu(total[:, :LANES]) * total[:, LANES:] * scale
            inner[:, at * units + tile : at * units + tile + LANES] = value.astype(BF16)

    copy.wait()
    for start in range(0, width, STEP):
        mat = jnp.concatenate([own[2][:, start : start + STEP], others[2][:, start : start + STEP]], axis=0)
        value = jnp.dot(inner[...], mat, preferred_element_type=F32)
        at = 0
        for out in outs:
            out[:, start : start + STEP] = value[at : at + out.shape[0]].astype(BF16)
            at += out.shape[0]


def expert_rows(parts, outs, width, mine, experts, weights):
    rows = sum(part.shape[0] for part in parts)
    units = weights[0].shape[1]
    *weights, last = weights
    weights = [pltpu.with_memory_space_constraint(w, pltpu.VMEM) for w in weights]
    return call(
        functools.partial(expert_kernel, experts, len(parts)),
        tuple(jax.ShapeDtypeStruct((n, width), BF16) for n in outs),
        [SMEM] + [VMEM] * (len(parts) + len(weights)) + [HBM],
        (mine, *parts, *weights, last),
        [
            pltpu.VMEM((rows, width), BF16),
            pltpu.VMEM((rows, 2 * units), BF16),
            pltpu.VMEM(last.shape, BF16),
            pltpu.SemaphoreType.DMA,
        ],
        limit=16,
        flops=6 * rows * width * 2 * units,
    )


def permute(value, devices, flip_of):
    pairs = [(device, device ^ flip_of(device)) for device in range(devices)]
    return lax.ppermute(value, "expert", pairs)


def level_flip(step, device):
    return 8 * (step + device % 2)


def first_flip(device):
    return 2 if device % 2 == 0 else 4


def second_flip(device):
    return 4 if device % 2 == 0 else 2


def join_kernel(a, b, out):
    for start in range(0, out.shape[1], LANES):
        at = pl.ds(start, LANES)
        out[:, at] = jnp.concatenate([a[:, at].astype(F32), b[:, at].astype(F32)], axis=0).astype(BF16)


def join(a, b):
    out = jax.ShapeDtypeStruct((2 * a.shape[0], a.shape[1]), BF16)
    return call(join_kernel, out, [VMEM] * 2, (a, b))


def add_kernel(a, b, out):
    rows, width = out.shape
    for start in range(0, width, STEP):
        at = pl.ds(start, STEP)
        out[:, at] = (a[:, at].astype(F32) + b[:, at].astype(F32)[-rows:]).astype(BF16)


def add(a, b, cost=0):
    return call(add_kernel, jax.ShapeDtypeStruct(a.shape, BF16), [VMEM] * 2, (a, b), moved=cost)


def per_device(hidden, expert_ids, gate_raw, w_gate, w_up, w_down):
    devices = lax.axis_size("expert")
    experts = devices // 2
    levels = devices // 8
    rows, width = hidden.shape
    mine = (lax.axis_index("expert") // 2).reshape(1)
    go = lambda value, flip: permute(value, devices, flip)

    own = fold_rows(hidden, expert_ids, gate_raw, experts)

    weights = [w_gate[0], w_up[0], w_down[0]]

    both = pair_rows((own, go(own, lambda device: 1)), width, experts)
    weights, both = lax.optimization_barrier((weights, both))
    others = [go(w, lambda device: 1) for w in weights]
    far = [go(both, lambda device, s=step: level_flip(s, device)) for step in range(2, levels, 2)]
    far = far[0] if len(far) == 1 else jnp.concatenate(far, axis=0)
    own_first = go(own, first_flip)
    own_second = go(join(own, own_first), second_flip)
    far, own_second = lax.optimization_barrier((far, own_second))
    far_first = go(far, first_flip)
    far_second = go(far, second_flip)
    near = pair_rows((own, own_first, own_second), width, experts)
    near_other = go(near, lambda device: 8)
    weights, far_first = lax.optimization_barrier((weights, far_first))
    far_third = go(far_first, second_flip)
    weights = list(fetch(weights + others[:2])) + others[2:]

    many, more = far.shape[0], near.shape[0]
    near, near_other, far, far_first, far_second, far_third = expert_rows(
        (near, near_other, far, far_first, far_second, far_third),
        (more, more, many, many, many, many),
        width,
        mine,
        experts,
        weights,
    )

    far_third = go(far_third, second_flip)
    far_second = go(far_second, second_flip)
    near_other = go(near_other, lambda device: 8)
    far_first = go(add(far_first, far_third, COST), first_flip)
    far = split_rows((far, far_second, far_first), [(block,) for block in range(levels - 2)], COST)
    far = [
        go(block, lambda device, s=step, twin=twin: level_flip(s, device) + twin)
        for block, (step, twin) in zip(far, [(s, t) for s in range(2, levels, 2) for t in range(2)])
    ]
    own, own_first, own_second = split_rows((near, near_other), ((0,), (1,), (2, 3)))
    own_second = go(own_second, second_flip)
    own_first = go(add(own_first, own_second), first_flip)
    return last_rows([own, own_first, own_second] + far, rows, width)


def solution(mesh):
    placed = (
        P(("groups", "expert"), None),
        P(("groups", "expert"), None),
        P(("groups", "expert"), None),
        P("expert", None, None),
        P("expert", None, None),
        P("expert", None, None),
    )
    return jax.shard_map(
        per_device,
        mesh=mesh,
        in_specs=placed,
        out_specs=P(("groups", "expert"), None),
        check_vma=False,
    )
```

```python
import functools
import math

import jax
import jax.numpy as jnp
from jax import lax
from jax.experimental import pallas as pl
from jax.experimental.pallas import tpu as pltpu
from jax.sharding import PartitionSpec as P

BF16 = jnp.bfloat16
F32 = jnp.float32
TILE = 8
HALF_TILE = 4
LANES = 128
STEP = 512
PIECES = 4
ROOM = 3
VMEM = pl.BlockSpec(memory_space=pltpu.VMEM)
SMEM = pl.BlockSpec(memory_space=pltpu.SMEM)
HBM = pl.BlockSpec(memory_space=pltpu.HBM)


def call(kernel, out_shape, in_specs, args, scratch=(), room=1, held=0, flops=0):
    args = [
        pltpu.with_memory_space_constraint(arg, pltpu.HBM) if spec is HBM else arg
        for arg, spec in zip(args, in_specs)
    ]
    single = not isinstance(out_shape, tuple)
    outs = (out_shape,) if single else out_shape
    arrays = [arg for arg, spec in zip(args, in_specs) if spec is VMEM] + [*outs, *scratch]
    size = sum(math.prod(array.shape) * array.dtype.itemsize for array in arrays if hasattr(array.dtype, "itemsize"))
    return pl.pallas_call(
        kernel,
        out_shape=out_shape,
        in_specs=in_specs,
        out_specs=VMEM if single else (VMEM,) * len(out_shape),
        scratch_shapes=scratch,
        compiler_params=pltpu.CompilerParams(vmem_limit_bytes=size - held + (room << 20)),
        cost_estimate=pl.CostEstimate(flops=flops, bytes_accessed=0, transcendentals=0),
    )(*args)


def size_of(arrays):
    return sum(math.prod(array.shape) * array.dtype.itemsize for array in arrays)


def upper_rows(shape):
    return lax.broadcasted_iota(jnp.int32, shape, 0) < HALF_TILE


def swap(tile):
    return pltpu.roll(tile, HALF_TILE, 0)


def fold_kernel(experts, *refs):
    sources, out, (ids, gate, hidden, turned, sems) = refs[:3], refs[3], refs[4:]
    copies = [
        pltpu.make_async_copy(source, target, sems.at[i])
        for i, (source, target) in enumerate(zip(sources, (ids, gate, hidden)))
    ]
    for copy in copies:
        copy.start()
    copies[0].wait()
    copies[1].wait()
    rows, width = hidden.shape
    half = width // 2
    top = ids.shape[0]
    lanes = turned.shape[0]
    raw = gate[...]
    weight = raw / jnp.sum(raw, axis=0, keepdims=True)
    expert = lax.broadcasted_iota(jnp.int32, (lanes, rows), 0) % experts
    dense = jnp.zeros((lanes, rows), F32)
    for t in range(top):
        dense = jnp.where(ids[t : t + 1, :] == expert, weight[t : t + 1, :], dense)
    turned[:, :rows] = dense
    dense = turned[...].T
    high = dense.astype(BF16).astype(F32)
    first, last = high[:TILE], high[TILE : 2 * TILE]
    low_first, low_last = dense[:TILE] - first, dense[TILE : 2 * TILE] - last
    upper = upper_rows((TILE, lanes))
    last = jnp.where(upper, last, swap(last))
    low_last = jnp.where(upper, low_last, swap(low_last))
    role = lax.broadcasted_iota(jnp.int32, (TILE, lanes), 1) // experts
    side = jnp.where(
        role == 0,
        first,
        jnp.where(role == 1, low_first, jnp.where(role == 2, last, jnp.where(role == 3, low_last, 0.0))),
    )
    out[:, width + half :] = side.astype(BF16)
    copies[2].wait()
    out[:, :width] = hidden[:TILE, :]
    rest = hidden[TILE:, :].astype(F32)
    out[:, width : width + half] = jnp.concatenate([rest[:, :half], rest[:, half:]], axis=0).astype(BF16)


def fold_rows(hidden, expert_ids, gate_raw, experts):
    rows, width = hidden.shape
    lanes = -(-4 * experts // LANES) * LANES
    out = jax.ShapeDtypeStruct((TILE, width + width // 2 + lanes), BF16)
    return call(
        functools.partial(fold_kernel, experts),
        out,
        [HBM] * 3,
        (expert_ids.T, gate_raw.T, hidden),
        [
            pltpu.VMEM(expert_ids.T.shape, expert_ids.dtype),
            pltpu.VMEM(gate_raw.T.shape, F32),
            pltpu.VMEM(hidden.shape, BF16),
            pltpu.VMEM((lanes, LANES), F32),
            pltpu.SemaphoreType.DMA((3,)),
        ],
    )


def pair_kernel(experts, width, *refs):
    parts, out = refs[:-1], refs[-1]
    half = width // 2

    def tiles(start, size):
        values = [part[:, start : start + size].astype(F32) for part in parts]
        return [value[at : at + TILE] for value in values for at in range(0, value.shape[0], TILE)]

    lanes = out.shape[1] - width

    def put(at, size, firsts, lasts):
        rows = [row for a, b, last in zip(firsts[::2], firsts[1::2], lasts) for row in (a, b, last)]
        out[:, at : at + size] = jnp.concatenate(rows, axis=0).astype(BF16)

    upper = upper_rows((TILE, STEP))
    for start in range(0, half, STEP):
        rest = tiles(width + start, STEP)
        for at, turn in ((start, False), (half + start, True)):
            lasts = [
                jnp.where(upper, swap(a) if turn else a, b if turn else swap(b))
                for a, b in zip(rest[::2], rest[1::2])
            ]
            put(at, STEP, tiles(at, STEP), lasts)
    side = tiles(width + half, lanes)
    first = lax.broadcasted_iota(jnp.int32, (TILE, lanes), 1) < 2 * experts
    upper = upper_rows((TILE, lanes))
    put(
        width,
        lanes,
        [jnp.where(first, value, 0.0) for value in side],
        [jnp.where(first, 0.0, jnp.where(upper, a, b)) for a, b in zip(side[::2], side[1::2])],
    )


def pair_rows(parts, width, experts):
    lanes = parts[0].shape[1] - width - width // 2
    rows = sum(part.shape[0] for part in parts)
    out = jax.ShapeDtypeStruct((rows + rows // 2, width + lanes), BF16)
    return call(functools.partial(pair_kernel, experts, width), out, [VMEM] * len(parts), parts)


def split_kernel(order, *refs):
    parts, outs = refs[: -len(order)], refs[-len(order) :]
    rows, width = parts[0].shape
    half = width // 2
    upper = upper_rows((TILE, STEP))

    def tiles(at):
        total = sum(part[:, at : at + STEP].astype(F32)[:rows] for part in parts)
        return [total[row : row + TILE] for row in range(0, rows, TILE)]

    def put(at, values):
        for out, blocks in zip(outs, order):
            value = jnp.concatenate([values[block] for block in blocks], axis=0)
            out[:, at : at + STEP] = value.astype(BF16)

    for start in range(0, half, STEP):
        low, high = tiles(start), tiles(half + start)
        rest = []
        for a, b in zip(low[2::3], high[2::3]):
            rest += [jnp.where(upper, a, swap(b)), jnp.where(upper, swap(a), b)]
        put(start, [tile for i, tile in enumerate(low) if i % 3 < 2])
        put(half + start, [tile for i, tile in enumerate(high) if i % 3 < 2])
        put(width + start, rest)


def split_rows(parts, order):
    width = parts[0].shape[1]
    shapes = tuple(jax.ShapeDtypeStruct((TILE * len(blocks), width + width // 2), BF16) for blocks in order)
    return call(functools.partial(split_kernel, order), shapes, [VMEM] * len(parts), parts)


def last_kernel(*refs):
    parts, out = refs[:-1], refs[-1]
    rows, width = out.shape
    half = width // 2
    for start in range(0, half, STEP):
        low, high, rest = (
            sum(part[:, at : at + STEP].astype(F32)[:TILE] for part in parts)
            for at in (start, half + start, width + start)
        )
        out[:, start : start + STEP] = jnp.concatenate([low, rest[:HALF_TILE]], axis=0).astype(BF16)
        out[:, half + start : half + start + STEP] = jnp.concatenate(
            [high, rest[HALF_TILE:]], axis=0
        ).astype(BF16)


def last_rows(parts, rows, width):
    return call(last_kernel, jax.ShapeDtypeStruct((rows, width), BF16), [VMEM] * len(parts), parts)


def fetch_kernel(*refs):
    count = len(refs) // 2
    sources, targets, sems = refs[:count], refs[count:-1], refs[-1]
    copies = []
    for i, (source, target) in enumerate(zip(sources, targets)):
        rows = source.shape[0] // PIECES
        for j in range(PIECES):
            at = pl.ds(j * rows, rows)
            copies.append(pltpu.make_async_copy(source.at[at], target.at[at], sems.at[i, j]))
    for copy in copies:
        copy.start()
    for copy in copies:
        copy.wait()


def fetch(arrays):
    return call(
        fetch_kernel,
        tuple(pltpu.VMEM(w.shape, w.dtype) for w in arrays),
        [HBM] * len(arrays),
        arrays,
        [pltpu.SemaphoreType.DMA((len(arrays), PIECES))],
        held=size_of(arrays),
    )


def expert_kernel(experts, count, mine, *refs):
    parts, own, others = refs[:count], refs[count : count + 3], refs[count + 3 : count + 6]
    outs, (xs, inner) = refs[count + 6 : -2], refs[-2:]
    width = outs[0].shape[1]
    units = own[0].shape[1]

    for start in range(0, width, STEP):
        xs[:, start : start + STEP] = jnp.concatenate(
            [part[:, start : start + STEP].astype(F32) for part in parts], axis=0
        ).astype(BF16)
    side = jnp.concatenate([part[:, width:].astype(F32) for part in parts], axis=0)
    lane = lax.broadcasted_iota(jnp.int32, side.shape, 1)
    scale = jnp.sum(jnp.where(lane % experts == mine[0], side, 0.0), axis=1, keepdims=True)

    for at, (gate, up, unused) in enumerate((own, others)):
        for tile in range(0, units, LANES):
            piece = slice(tile, tile + LANES)
            total = jnp.dot(
                xs[...],
                jnp.concatenate([gate[:, piece], up[:, piece]], axis=1),
                preferred_element_type=F32,
            )
            value = jax.nn.silu(total[:, :LANES]) * total[:, LANES:] * scale
            inner[:, at * units + tile : at * units + tile + LANES] = value.astype(BF16)

    for start in range(0, width, STEP):
        mat = jnp.concatenate([own[2][:, start : start + STEP], others[2][:, start : start + STEP]], axis=0)
        value = jnp.dot(inner[...], mat, preferred_element_type=F32)
        at = 0
        for out in outs:
            out[:, start : start + STEP] = value[at : at + out.shape[0]].astype(BF16)
            at += out.shape[0]


def expert_rows(parts, outs, width, mine, experts, weights):
    rows = sum(part.shape[0] for part in parts)
    units = weights[0].shape[1]
    weights = [pltpu.with_memory_space_constraint(w, pltpu.VMEM) for w in weights]
    return call(
        functools.partial(expert_kernel, experts, len(parts)),
        tuple(jax.ShapeDtypeStruct((n, width), BF16) for n in outs),
        [SMEM] + [VMEM] * (len(parts) + len(weights)),
        (mine, *parts, *weights),
        [
            pltpu.VMEM((rows, width), BF16),
            pltpu.VMEM((rows, 2 * units), BF16),
        ],
        room=ROOM,
        held=size_of(weights),
        flops=6 * rows * width * 2 * units,
    )


def permute(value, devices, flip_of):
    pairs = [(device, device ^ flip_of(device)) for device in range(devices)]
    return lax.ppermute(value, "expert", pairs)


def level_flip(step, device):
    return 8 * (step + device % 2)


def first_flip(device):
    return 2 if device % 2 == 0 else 4


def second_flip(device):
    return 4 if device % 2 == 0 else 2


def join_kernel(a, b, out):
    for start in range(0, out.shape[1], LANES):
        at = pl.ds(start, LANES)
        out[:, at] = jnp.concatenate([a[:, at].astype(F32), b[:, at].astype(F32)], axis=0).astype(BF16)


def join(a, b):
    out = jax.ShapeDtypeStruct((2 * a.shape[0], a.shape[1]), BF16)
    return call(join_kernel, out, [VMEM] * 2, (a, b))


def add_kernel(a, b, out):
    rows, width = out.shape
    for start in range(0, width, STEP):
        at = pl.ds(start, STEP)
        out[:, at] = (a[:, at].astype(F32) + b[:, at].astype(F32)[-rows:]).astype(BF16)


def add(a, b):
    return call(add_kernel, jax.ShapeDtypeStruct(a.shape, BF16), [VMEM] * 2, (a, b))


def per_device(hidden, expert_ids, gate_raw, w_gate, w_up, w_down):
    devices = lax.axis_size("expert")
    experts = devices // 2
    levels = devices // 8
    rows, width = hidden.shape
    mine = (lax.axis_index("expert") // 2).reshape(1)
    go = lambda value, flip: permute(value, devices, flip)

    own = fold_rows(hidden, expert_ids, gate_raw, experts)

    weights = [w_gate[0], w_up[0], w_down[0]]

    both = pair_rows((own, go(own, lambda device: 1)), width, experts)
    weights, both = lax.optimization_barrier((weights, both))
    others = [go(w, lambda device: 1) for w in weights[:2]]
    far = [go(both, lambda device, s=step: level_flip(s, device)) for step in range(2, levels, 2)]
    far = far[0] if len(far) == 1 else jnp.concatenate(far, axis=0)
    own_first = go(own, first_flip)
    plane = (own, own_first, go(join(own, own_first), second_flip))
    weights, own_first = lax.optimization_barrier((weights, own_first))
    weights = list(fetch(weights[:1])) + weights[1:]
    far, plane, weights = lax.optimization_barrier((far, plane, weights))
    others.append(go(weights[2], lambda device: 1))
    far_first = go(far, first_flip)
    far_second = go(far, second_flip)
    near = pair_rows(plane, width, experts)
    near_other = go(near, lambda device: 8)
    others, far_first = lax.optimization_barrier((others, far_first))
    far_third = go(far_first, second_flip)
    weights = weights[:1] + list(fetch(weights[1:] + others))

    many, more = far.shape[0], near.shape[0]
    near, near_other, far, far_first, far_second, far_third = expert_rows(
        (near, near_other, far, far_first, far_second, far_third),
        (more, more, many, many, many, many),
        width,
        mine,
        experts,
        weights,
    )

    far_third = go(far_third, second_flip)
    far_second = go(far_second, second_flip)
    near_other = go(near_other, lambda device: 8)
    far_first = go(add(far_first, far_third), first_flip)
    far = split_rows((far, far_second, far_first), [(block,) for block in range(levels - 2)])
    far = [
        go(block, lambda device, s=step, twin=twin: level_flip(s, device) + twin)
        for block, (step, twin) in zip(far, [(s, t) for s in range(2, levels, 2) for t in range(2)])
    ]
    own, own_first, own_second = split_rows((near, near_other), ((0,), (1,), (2, 3)))
    own_second = go(own_second, second_flip)
    own_first = go(add(own_first, own_second), first_flip)
    return last_rows([own, own_first, own_second] + far, rows, width)


def solution(mesh):
    placed = (
        P(("groups", "expert"), None),
        P(("groups", "expert"), None),
        P(("groups", "expert"), None),
        P("expert", None, None),
        P("expert", None, None),
        P("expert", None, None),
    )
    return jax.shard_map(
        per_device,
        mesh=mesh,
        in_specs=placed,
        out_specs=P(("groups", "expert"), None),
        check_vma=False,
    )
```

```python
import functools
import math

import jax
import jax.numpy as jnp
from jax import lax
from jax.experimental import pallas as pl
from jax.experimental.pallas import tpu as pltpu
from jax.sharding import PartitionSpec as P

BF16 = jnp.bfloat16
F32 = jnp.float32
TILE = 8
HALF_TILE = 4
LANES = 128
STEP = 512
PIECES = 4
ROOM = 3
VMEM = pl.BlockSpec(memory_space=pltpu.VMEM)
SMEM = pl.BlockSpec(memory_space=pltpu.SMEM)
HBM = pl.BlockSpec(memory_space=pltpu.HBM)


def call(kernel, out_shape, in_specs, args, scratch=(), room=1, held=0, flops=0):
    args = [
        pltpu.with_memory_space_constraint(arg, pltpu.HBM) if spec is HBM else arg
        for arg, spec in zip(args, in_specs)
    ]
    single = not isinstance(out_shape, tuple)
    outs = (out_shape,) if single else out_shape
    arrays = [arg for arg, spec in zip(args, in_specs) if spec is VMEM] + [*outs, *scratch]
    size = sum(math.prod(array.shape) * array.dtype.itemsize for array in arrays if hasattr(array.dtype, "itemsize"))
    return pl.pallas_call(
        kernel,
        out_shape=out_shape,
        in_specs=in_specs,
        out_specs=VMEM if single else (VMEM,) * len(out_shape),
        scratch_shapes=scratch,
        compiler_params=pltpu.CompilerParams(vmem_limit_bytes=size - held + (room << 20)),
        cost_estimate=pl.CostEstimate(flops=flops, bytes_accessed=0, transcendentals=0),
    )(*args)


def size_of(arrays):
    return sum(math.prod(array.shape) * array.dtype.itemsize for array in arrays)


def upper_rows(shape):
    return lax.broadcasted_iota(jnp.int32, shape, 0) < HALF_TILE


def swap(tile):
    return pltpu.roll(tile, HALF_TILE, 0)


def fold_kernel(experts, *refs):
    sources, out, (ids, gate, hidden, turned, sems) = refs[:3], refs[3], refs[4:]
    copies = [
        pltpu.make_async_copy(source, target, sems.at[i])
        for i, (source, target) in enumerate(zip(sources, (ids, gate, hidden)))
    ]
    for copy in copies:
        copy.start()
    copies[0].wait()
    copies[1].wait()
    rows, width = hidden.shape
    half = width // 2
    top = ids.shape[0]
    lanes = turned.shape[0]
    raw = gate[...]
    weight = raw / jnp.sum(raw, axis=0, keepdims=True)
    expert = lax.broadcasted_iota(jnp.int32, (lanes, rows), 0) % experts
    dense = jnp.zeros((lanes, rows), F32)
    for t in range(top):
        dense = jnp.where(ids[t : t + 1, :] == expert, weight[t : t + 1, :], dense)
    turned[:, :rows] = dense
    dense = turned[...].T
    high = dense.astype(BF16).astype(F32)
    first, last = high[:TILE], high[TILE : 2 * TILE]
    low_first, low_last = dense[:TILE] - first, dense[TILE : 2 * TILE] - last
    upper = upper_rows((TILE, lanes))
    last = jnp.where(upper, last, swap(last))
    low_last = jnp.where(upper, low_last, swap(low_last))
    role = lax.broadcasted_iota(jnp.int32, (TILE, lanes), 1) // experts
    side = jnp.where(
        role == 0,
        first,
        jnp.where(role == 1, low_first, jnp.where(role == 2, last, jnp.where(role == 3, low_last, 0.0))),
    )
    out[:, width + half :] = side.astype(BF16)
    copies[2].wait()
    out[:, :width] = hidden[:TILE, :]
    rest = hidden[TILE:, :].astype(F32)
    out[:, width : width + half] = jnp.concatenate([rest[:, :half], rest[:, half:]], axis=0).astype(BF16)


def fold_rows(hidden, expert_ids, gate_raw, experts):
    rows, width = hidden.shape
    lanes = -(-4 * experts // LANES) * LANES
    out = jax.ShapeDtypeStruct((TILE, width + width // 2 + lanes), BF16)
    return call(
        functools.partial(fold_kernel, experts),
        out,
        [HBM] * 3,
        (expert_ids.T, gate_raw.T, hidden),
        [
            pltpu.VMEM(expert_ids.T.shape, expert_ids.dtype),
            pltpu.VMEM(gate_raw.T.shape, F32),
            pltpu.VMEM(hidden.shape, BF16),
            pltpu.VMEM((lanes, LANES), F32),
            pltpu.SemaphoreType.DMA((3,)),
        ],
    )


def pair_kernel(experts, width, *refs):
    parts, out = refs[:-1], refs[-1]
    half = width // 2

    def tiles(start, size):
        values = [part[:, start : start + size].astype(F32) for part in parts]
        return [value[at : at + TILE] for value in values for at in range(0, value.shape[0], TILE)]

    lanes = out.shape[1] - width

    def put(at, size, firsts, lasts):
        rows = [row for a, b, last in zip(firsts[::2], firsts[1::2], lasts) for row in (a, b, last)]
        out[:, at : at + size] = jnp.concatenate(rows, axis=0).astype(BF16)

    upper = upper_rows((TILE, STEP))
    for start in range(0, half, STEP):
        rest = tiles(width + start, STEP)
        for at, turn in ((start, False), (half + start, True)):
            lasts = [
                jnp.where(upper, swap(a) if turn else a, b if turn else swap(b))
                for a, b in zip(rest[::2], rest[1::2])
            ]
            put(at, STEP, tiles(at, STEP), lasts)
    side = tiles(width + half, lanes)
    first = lax.broadcasted_iota(jnp.int32, (TILE, lanes), 1) < 2 * experts
    upper = upper_rows((TILE, lanes))
    put(
        width,
        lanes,
        [jnp.where(first, value, 0.0) for value in side],
        [jnp.where(first, 0.0, jnp.where(upper, a, b)) for a, b in zip(side[::2], side[1::2])],
    )


def pair_rows(parts, width, experts):
    lanes = parts[0].shape[1] - width - width // 2
    rows = sum(part.shape[0] for part in parts)
    out = jax.ShapeDtypeStruct((rows + rows // 2, width + lanes), BF16)
    return call(functools.partial(pair_kernel, experts, width), out, [VMEM] * len(parts), parts)


def split_kernel(order, *refs):
    parts, outs = refs[: -len(order)], refs[-len(order) :]
    rows, width = parts[0].shape
    half = width // 2
    upper = upper_rows((TILE, STEP))

    def tiles(at):
        total = sum(part[:, at : at + STEP].astype(F32)[:rows] for part in parts)
        return [total[row : row + TILE] for row in range(0, rows, TILE)]

    def put(at, values):
        for out, blocks in zip(outs, order):
            value = jnp.concatenate([values[block] for block in blocks], axis=0)
            out[:, at : at + STEP] = value.astype(BF16)

    for start in range(0, half, STEP):
        low, high = tiles(start), tiles(half + start)
        rest = []
        for a, b in zip(low[2::3], high[2::3]):
            rest += [jnp.where(upper, a, swap(b)), jnp.where(upper, swap(a), b)]
        put(start, [tile for i, tile in enumerate(low) if i % 3 < 2])
        put(half + start, [tile for i, tile in enumerate(high) if i % 3 < 2])
        put(width + start, rest)


def split_rows(parts, order):
    width = parts[0].shape[1]
    shapes = tuple(jax.ShapeDtypeStruct((TILE * len(blocks), width + width // 2), BF16) for blocks in order)
    return call(functools.partial(split_kernel, order), shapes, [VMEM] * len(parts), parts)


def last_kernel(*refs):
    parts, out = refs[:-1], refs[-1]
    rows, width = out.shape
    half = width // 2
    for start in range(0, half, STEP):
        low, high, rest = (
            sum(part[:, at : at + STEP].astype(F32)[:TILE] for part in parts)
            for at in (start, half + start, width + start)
        )
        out[:, start : start + STEP] = jnp.concatenate([low, rest[:HALF_TILE]], axis=0).astype(BF16)
        out[:, half + start : half + start + STEP] = jnp.concatenate(
            [high, rest[HALF_TILE:]], axis=0
        ).astype(BF16)


def last_rows(parts, rows, width):
    return call(last_kernel, jax.ShapeDtypeStruct((rows, width), BF16), [VMEM] * len(parts), parts)


def fetch_kernel(*refs):
    count = len(refs) // 2
    sources, targets, sems = refs[:count], refs[count:-1], refs[-1]
    copies = []
    for i, (source, target) in enumerate(zip(sources, targets)):
        rows = source.shape[0] // PIECES
        for j in range(PIECES):
            at = pl.ds(j * rows, rows)
            copies.append(pltpu.make_async_copy(source.at[at], target.at[at], sems.at[i, j]))
    for copy in copies:
        copy.start()
    for copy in copies:
        copy.wait()


def fetch(arrays):
    return call(
        fetch_kernel,
        tuple(pltpu.VMEM(w.shape, w.dtype) for w in arrays),
        [HBM] * len(arrays),
        arrays,
        [pltpu.SemaphoreType.DMA((len(arrays), PIECES))],
        held=size_of(arrays),
    )


def expert_kernel(experts, count, mine, *refs):
    parts, own, others = refs[:count], refs[count : count + 3], refs[count + 3 : count + 6]
    outs, (xs, inner) = refs[count + 6 : -2], refs[-2:]
    width = outs[0].shape[1]
    units = own[0].shape[1]

    for start in range(0, width, STEP):
        xs[:, start : start + STEP] = jnp.concatenate(
            [part[:, start : start + STEP].astype(F32) for part in parts], axis=0
        ).astype(BF16)
    side = jnp.concatenate([part[:, width:].astype(F32) for part in parts], axis=0)
    lane = lax.broadcasted_iota(jnp.int32, side.shape, 1)
    scale = jnp.sum(jnp.where(lane % experts == mine[0], side, 0.0), axis=1, keepdims=True)

    for at, (gate, up, unused) in enumerate((own, others)):
        for tile in range(0, units, LANES):
            piece = slice(tile, tile + LANES)
            total = jnp.dot(
                xs[...],
                jnp.concatenate([gate[:, piece], up[:, piece]], axis=1),
                preferred_element_type=F32,
            )
            value = jax.nn.silu(total[:, :LANES]) * total[:, LANES:] * scale
            inner[:, at * units + tile : at * units + tile + LANES] = value.astype(BF16)

    for start in range(0, width, STEP):
        mat = jnp.concatenate([own[2][:, start : start + STEP], others[2][:, start : start + STEP]], axis=0)
        value = jnp.dot(inner[...], mat, preferred_element_type=F32)
        at = 0
        for out in outs:
            out[:, start : start + STEP] = value[at : at + out.shape[0]].astype(BF16)
            at += out.shape[0]


def expert_rows(parts, outs, width, mine, experts, weights):
    rows = sum(part.shape[0] for part in parts)
    units = weights[0].shape[1]
    weights = [pltpu.with_memory_space_constraint(w, pltpu.VMEM) for w in weights]
    return call(
        functools.partial(expert_kernel, experts, len(parts)),
        tuple(jax.ShapeDtypeStruct((n, width), BF16) for n in outs),
        [SMEM] + [VMEM] * (len(parts) + len(weights)),
        (mine, *parts, *weights),
        [
            pltpu.VMEM((rows, width), BF16),
            pltpu.VMEM((rows, 2 * units), BF16),
        ],
        room=ROOM,
        held=size_of(weights),
        flops=6 * rows * width * 2 * units,
    )


def permute(value, devices, flip_of):
    pairs = [(device, device ^ flip_of(device)) for device in range(devices)]
    return lax.ppermute(value, "expert", pairs)


def level_flip(step, device):
    return 8 * (step + device % 2)


def first_flip(device):
    return 2 if device % 2 == 0 else 4


def second_flip(device):
    return 4 if device % 2 == 0 else 2


def join_kernel(a, b, out):
    for start in range(0, out.shape[1], LANES):
        at = pl.ds(start, LANES)
        out[:, at] = jnp.concatenate([a[:, at].astype(F32), b[:, at].astype(F32)], axis=0).astype(BF16)


def join(a, b):
    out = jax.ShapeDtypeStruct((2 * a.shape[0], a.shape[1]), BF16)
    return call(join_kernel, out, [VMEM] * 2, (a, b))


def add_kernel(a, b, out):
    rows, width = out.shape
    for start in range(0, width, STEP):
        at = pl.ds(start, STEP)
        out[:, at] = (a[:, at].astype(F32) + b[:, at].astype(F32)[-rows:]).astype(BF16)


def add(a, b):
    return call(add_kernel, jax.ShapeDtypeStruct(a.shape, BF16), [VMEM] * 2, (a, b))


def per_device(hidden, expert_ids, gate_raw, w_gate, w_up, w_down):
    devices = lax.axis_size("expert")
    experts = devices // 2
    levels = devices // 8
    rows, width = hidden.shape
    mine = (lax.axis_index("expert") // 2).reshape(1)
    go = lambda value, flip: permute(value, devices, flip)

    own = fold_rows(hidden, expert_ids, gate_raw, experts)

    weights = [w_gate[0], w_up[0], w_down[0]]

    both = pair_rows((own, go(own, lambda device: 1)), width, experts)
    weights, both = lax.optimization_barrier((weights, both))
    others = [go(w, lambda device: 1) for w in weights[:2]]
    far = [go(both, lambda device, s=step: level_flip(s, device)) for step in range(2, levels, 2)]
    far = far[0] if len(far) == 1 else jnp.concatenate(far, axis=0)
    own_first = go(own, first_flip)
    plane = (own, own_first, go(join(own, own_first), second_flip))
    weights, own_first = lax.optimization_barrier((weights, own_first))
    weights = list(fetch(weights[:1])) + weights[1:]
    far, plane, weights = lax.optimization_barrier((far, plane, weights))
    others.append(go(weights[2], lambda device: 1))
    far_first = go(far, first_flip)
    far_second = go(far, second_flip)
    near = pair_rows(plane, width, experts)
    near_other = go(near, lambda device: 8)
    weights, far_first = lax.optimization_barrier((weights, far_first))
    far_third = go(far_first, second_flip)
    weights = weights[:1] + list(fetch(weights[1:] + others))

    many, more = far.shape[0], near.shape[0]
    near, near_other, far, far_first, far_second, far_third = expert_rows(
        (near, near_other, far, far_first, far_second, far_third),
        (more, more, many, many, many, many),
        width,
        mine,
        experts,
        weights,
    )

    far_third = go(far_third, second_flip)
    far_second = go(far_second, second_flip)
    near_other = go(near_other, lambda device: 8)
    far_first = go(add(far_first, far_third), first_flip)
    far = split_rows((far, far_second, far_first), [(block,) for block in range(levels - 2)])
    far = [
        go(block, lambda device, s=step, twin=twin: level_flip(s, device) + twin)
        for block, (step, twin) in zip(far, [(s, t) for s in range(2, levels, 2) for t in range(2)])
    ]
    own, own_first, own_second = split_rows((near, near_other), ((0,), (1,), (2, 3)))
    own_second = go(own_second, second_flip)
    own_first = go(add(own_first, own_second), first_flip)
    return last_rows([own, own_first, own_second] + far, rows, width)


def solution(mesh):
    placed = (
        P(("groups", "expert"), None),
        P(("groups", "expert"), None),
        P(("groups", "expert"), None),
        P("expert", None, None),
        P("expert", None, None),
        P("expert", None, None),
    )
    return jax.shard_map(
        per_device,
        mesh=mesh,
        in_specs=placed,
        out_specs=P(("groups", "expert"), None),
        check_vma=False,
    )
```

```python
import functools
import math

import jax
import jax.numpy as jnp
from jax import lax
from jax.experimental import pallas as pl
from jax.experimental.pallas import tpu as pltpu
from jax.sharding import PartitionSpec as P

BF16 = jnp.bfloat16
F32 = jnp.float32
TILE = 8
HALF_TILE = 4
LANES = 128
STEP = 512
PIECES = 4
ROOM = 3
VMEM = pl.BlockSpec(memory_space=pltpu.VMEM)
SMEM = pl.BlockSpec(memory_space=pltpu.SMEM)
HBM = pl.BlockSpec(memory_space=pltpu.HBM)


def call(kernel, out_shape, in_specs, args, scratch=(), room=1, held=0, flops=0):
    args = [
        pltpu.with_memory_space_constraint(arg, pltpu.HBM) if spec is HBM else arg
        for arg, spec in zip(args, in_specs)
    ]
    single = not isinstance(out_shape, tuple)
    outs = (out_shape,) if single else out_shape
    arrays = [arg for arg, spec in zip(args, in_specs) if spec is VMEM] + [*outs, *scratch]
    size = sum(math.prod(array.shape) * array.dtype.itemsize for array in arrays if hasattr(array.dtype, "itemsize"))
    return pl.pallas_call(
        kernel,
        out_shape=out_shape,
        in_specs=in_specs,
        out_specs=VMEM if single else (VMEM,) * len(out_shape),
        scratch_shapes=scratch,
        compiler_params=pltpu.CompilerParams(vmem_limit_bytes=size - held + (room << 20)),
        cost_estimate=pl.CostEstimate(flops=flops, bytes_accessed=0, transcendentals=0),
    )(*args)


def size_of(arrays):
    return sum(math.prod(array.shape) * array.dtype.itemsize for array in arrays)


def upper_rows(shape):
    return lax.broadcasted_iota(jnp.int32, shape, 0) < HALF_TILE


def swap(tile):
    return pltpu.roll(tile, HALF_TILE, 0)


def fold_kernel(experts, *refs):
    sources, out, (ids, gate, hidden, turned, sems) = refs[:3], refs[3], refs[4:]
    copies = [
        pltpu.make_async_copy(source, target, sems.at[i])
        for i, (source, target) in enumerate(zip(sources, (ids, gate, hidden)))
    ]
    for copy in copies:
        copy.start()
    copies[0].wait()
    copies[1].wait()
    rows, width = hidden.shape
    half = width // 2
    top = ids.shape[0]
    lanes = turned.shape[0]
    raw = gate[...]
    weight = raw / jnp.sum(raw, axis=0, keepdims=True)
    expert = lax.broadcasted_iota(jnp.int32, (lanes, rows), 0) % experts
    dense = jnp.zeros((lanes, rows), F32)
    for t in range(top):
        dense = jnp.where(ids[t : t + 1, :] == expert, weight[t : t + 1, :], dense)
    turned[:, :rows] = dense
    dense = turned[...].T
    high = dense.astype(BF16).astype(F32)
    first, last = high[:TILE], high[TILE : 2 * TILE]
    low_first, low_last = dense[:TILE] - first, dense[TILE : 2 * TILE] - last
    upper = upper_rows((TILE, lanes))
    last = jnp.where(upper, last, swap(last))
    low_last = jnp.where(upper, low_last, swap(low_last))
    role = lax.broadcasted_iota(jnp.int32, (TILE, lanes), 1) // experts
    side = jnp.where(
        role == 0,
        first,
        jnp.where(role == 1, low_first, jnp.where(role == 2, last, jnp.where(role == 3, low_last, 0.0))),
    )
    out[:, width + half :] = side.astype(BF16)
    copies[2].wait()
    out[:, :width] = hidden[:TILE, :]
    rest = hidden[TILE:, :].astype(F32)
    out[:, width : width + half] = jnp.concatenate([rest[:, :half], rest[:, half:]], axis=0).astype(BF16)


def fold_rows(hidden, expert_ids, gate_raw, experts):
    rows, width = hidden.shape
    lanes = -(-4 * experts // LANES) * LANES
    out = jax.ShapeDtypeStruct((TILE, width + width // 2 + lanes), BF16)
    return call(
        functools.partial(fold_kernel, experts),
        out,
        [HBM] * 3,
        (expert_ids.T, gate_raw.T, hidden),
        [
            pltpu.VMEM(expert_ids.T.shape, expert_ids.dtype),
            pltpu.VMEM(gate_raw.T.shape, F32),
            pltpu.VMEM(hidden.shape, BF16),
            pltpu.VMEM((lanes, LANES), F32),
            pltpu.SemaphoreType.DMA((3,)),
        ],
    )


def pair_kernel(experts, width, *refs):
    parts, out = refs[:-1], refs[-1]
    half = width // 2

    def tiles(start, size):
        values = [part[:, start : start + size].astype(F32) for part in parts]
        return [value[at : at + TILE] for value in values for at in range(0, value.shape[0], TILE)]

    lanes = out.shape[1] - width

    def put(at, size, firsts, lasts):
        rows = [row for a, b, last in zip(firsts[::2], firsts[1::2], lasts) for row in (a, b, last)]
        out[:, at : at + size] = jnp.concatenate(rows, axis=0).astype(BF16)

    upper = upper_rows((TILE, STEP))
    for start in range(0, half, STEP):
        rest = tiles(width + start, STEP)
        for at, turn in ((start, False), (half + start, True)):
            lasts = [
                jnp.where(upper, swap(a) if turn else a, b if turn else swap(b))
                for a, b in zip(rest[::2], rest[1::2])
            ]
            put(at, STEP, tiles(at, STEP), lasts)
    side = tiles(width + half, lanes)
    first = lax.broadcasted_iota(jnp.int32, (TILE, lanes), 1) < 2 * experts
    upper = upper_rows((TILE, lanes))
    put(
        width,
        lanes,
        [jnp.where(first, value, 0.0) for value in side],
        [jnp.where(first, 0.0, jnp.where(upper, a, b)) for a, b in zip(side[::2], side[1::2])],
    )


def pair_rows(parts, width, experts):
    lanes = parts[0].shape[1] - width - width // 2
    rows = sum(part.shape[0] for part in parts)
    out = jax.ShapeDtypeStruct((rows + rows // 2, width + lanes), BF16)
    return call(functools.partial(pair_kernel, experts, width), out, [VMEM] * len(parts), parts)


def split_kernel(order, *refs):
    parts, outs = refs[: -len(order)], refs[-len(order) :]
    rows, width = parts[0].shape
    half = width // 2
    upper = upper_rows((TILE, STEP))

    def tiles(at):
        total = sum(part[:, at : at + STEP].astype(F32)[:rows] for part in parts)
        return [total[row : row + TILE] for row in range(0, rows, TILE)]

    def put(at, values):
        for out, blocks in zip(outs, order):
            value = jnp.concatenate([values[block] for block in blocks], axis=0)
            out[:, at : at + STEP] = value.astype(BF16)

    for start in range(0, half, STEP):
        low, high = tiles(start), tiles(half + start)
        rest = []
        for a, b in zip(low[2::3], high[2::3]):
            rest += [jnp.where(upper, a, swap(b)), jnp.where(upper, swap(a), b)]
        put(start, [tile for i, tile in enumerate(low) if i % 3 < 2])
        put(half + start, [tile for i, tile in enumerate(high) if i % 3 < 2])
        put(width + start, rest)


def split_rows(parts, order):
    width = parts[0].shape[1]
    shapes = tuple(jax.ShapeDtypeStruct((TILE * len(blocks), width + width // 2), BF16) for blocks in order)
    return call(functools.partial(split_kernel, order), shapes, [VMEM] * len(parts), parts)


def last_kernel(*refs):
    parts, out = refs[:-1], refs[-1]
    rows, width = out.shape
    half = width // 2
    for start in range(0, half, STEP):
        low, high, rest = (
            sum(part[:, at : at + STEP].astype(F32)[:TILE] for part in parts)
            for at in (start, half + start, width + start)
        )
        out[:, start : start + STEP] = jnp.concatenate([low, rest[:HALF_TILE]], axis=0).astype(BF16)
        out[:, half + start : half + start + STEP] = jnp.concatenate(
            [high, rest[HALF_TILE:]], axis=0
        ).astype(BF16)


def last_rows(parts, rows, width):
    return call(last_kernel, jax.ShapeDtypeStruct((rows, width), BF16), [VMEM] * len(parts), parts)


def fetch_kernel(*refs):
    count = len(refs) // 2
    sources, targets, sems = refs[:count], refs[count:-1], refs[-1]
    copies = []
    for i, (source, target) in enumerate(zip(sources, targets)):
        rows = source.shape[0] // PIECES
        for j in range(PIECES):
            at = pl.ds(j * rows, rows)
            copies.append(pltpu.make_async_copy(source.at[at], target.at[at], sems.at[i, j]))
    for copy in copies:
        copy.start()
    for copy in copies:
        copy.wait()


def fetch(arrays):
    return call(
        fetch_kernel,
        tuple(pltpu.VMEM(w.shape, w.dtype) for w in arrays),
        [HBM] * len(arrays),
        arrays,
        [pltpu.SemaphoreType.DMA((len(arrays), PIECES))],
        held=size_of(arrays),
    )


def expert_kernel(experts, count, mine, *refs):
    parts, own, others = refs[:count], refs[count : count + 3], refs[count + 3 : count + 6]
    outs, (xs, inner) = refs[count + 6 : -2], refs[-2:]
    width = outs[0].shape[1]
    units = own[0].shape[1]

    for start in range(0, width, STEP):
        xs[:, start : start + STEP] = jnp.concatenate(
            [part[:, start : start + STEP].astype(F32) for part in parts], axis=0
        ).astype(BF16)
    side = jnp.concatenate([part[:, width:].astype(F32) for part in parts], axis=0)
    lane = lax.broadcasted_iota(jnp.int32, side.shape, 1)
    scale = jnp.sum(jnp.where(lane % experts == mine[0], side, 0.0), axis=1, keepdims=True)

    for at, (gate, up, unused) in enumerate((own, others)):
        for tile in range(0, units, LANES):
            piece = slice(tile, tile + LANES)
            total = jnp.dot(
                xs[...],
                jnp.concatenate([gate[:, piece], up[:, piece]], axis=1),
                preferred_element_type=F32,
            )
            value = jax.nn.silu(total[:, :LANES]) * total[:, LANES:] * scale
            inner[:, at * units + tile : at * units + tile + LANES] = value.astype(BF16)

    for start in range(0, width, STEP):
        mat = jnp.concatenate([own[2][:, start : start + STEP], others[2][:, start : start + STEP]], axis=0)
        value = jnp.dot(inner[...], mat, preferred_element_type=F32)
        at = 0
        for out in outs:
            out[:, start : start + STEP] = value[at : at + out.shape[0]].astype(BF16)
            at += out.shape[0]


def expert_rows(parts, outs, width, mine, experts, weights):
    rows = sum(part.shape[0] for part in parts)
    units = weights[0].shape[1]
    weights = [pltpu.with_memory_space_constraint(w, pltpu.VMEM) for w in weights]
    return call(
        functools.partial(expert_kernel, experts, len(parts)),
        tuple(jax.ShapeDtypeStruct((n, width), BF16) for n in outs),
        [SMEM] + [VMEM] * (len(parts) + len(weights)),
        (mine, *parts, *weights),
        [
            pltpu.VMEM((rows, width), BF16),
            pltpu.VMEM((rows, 2 * units), BF16),
        ],
        room=ROOM,
        held=size_of(weights),
        flops=6 * rows * width * 2 * units,
    )


def permute(value, devices, flip_of):
    pairs = [(device, device ^ flip_of(device)) for device in range(devices)]
    return lax.ppermute(value, "expert", pairs)


def level_flip(step, device):
    return 8 * (step + device % 2)


def first_flip(device):
    return 2 if device % 2 == 0 else 4


def second_flip(device):
    return 4 if device % 2 == 0 else 2


def join_kernel(a, b, out):
    for start in range(0, out.shape[1], LANES):
        at = pl.ds(start, LANES)
        out[:, at] = jnp.concatenate([a[:, at].astype(F32), b[:, at].astype(F32)], axis=0).astype(BF16)


def join(a, b):
    out = jax.ShapeDtypeStruct((2 * a.shape[0], a.shape[1]), BF16)
    return call(join_kernel, out, [VMEM] * 2, (a, b))


def add_kernel(a, b, out):
    rows, width = out.shape
    for start in range(0, width, STEP):
        at = pl.ds(start, STEP)
        out[:, at] = (a[:, at].astype(F32) + b[:, at].astype(F32)[-rows:]).astype(BF16)


def add(a, b):
    return call(add_kernel, jax.ShapeDtypeStruct(a.shape, BF16), [VMEM] * 2, (a, b))


def per_device(hidden, expert_ids, gate_raw, w_gate, w_up, w_down):
    devices = lax.axis_size("expert")
    experts = devices // 2
    levels = devices // 8
    rows, width = hidden.shape
    mine = (lax.axis_index("expert") // 2).reshape(1)
    go = lambda value, flip: permute(value, devices, flip)

    own = fold_rows(hidden, expert_ids, gate_raw, experts)

    weights = [w_gate[0], w_up[0], w_down[0]]

    both = pair_rows((own, go(own, lambda device: 1)), width, experts)
    weights, both = lax.optimization_barrier((weights, both))
    others = [go(w, lambda device: 1) for w in weights[:2]]
    far = [go(both, lambda device, s=step: level_flip(s, device)) for step in range(2, levels, 2)]
    far = far[0] if len(far) == 1 else jnp.concatenate(far, axis=0)
    own_first = go(own, first_flip)
    plane = (own, own_first, go(join(own, own_first), second_flip))
    far, plane, weights = lax.optimization_barrier((far, plane, weights))
    others.append(go(weights[2], lambda device: 1))
    far_first = go(far, first_flip)
    far_second = go(far, second_flip)
    near = pair_rows(plane, width, experts)
    near_other = go(near, lambda device: 8)
    weights, far_first = lax.optimization_barrier((weights, far_first))
    far_third = go(far_first, second_flip)
    weights = list(fetch(weights + others))

    many, more = far.shape[0], near.shape[0]
    near, near_other, far, far_first, far_second, far_third = expert_rows(
        (near, near_other, far, far_first, far_second, far_third),
        (more, more, many, many, many, many),
        width,
        mine,
        experts,
        weights,
    )

    far_third = go(far_third, second_flip)
    far_second = go(far_second, second_flip)
    near_other = go(near_other, lambda device: 8)
    far_first = go(add(far_first, far_third), first_flip)
    far = split_rows((far, far_second, far_first), [(block,) for block in range(levels - 2)])
    far = [
        go(block, lambda device, s=step, twin=twin: level_flip(s, device) + twin)
        for block, (step, twin) in zip(far, [(s, t) for s in range(2, levels, 2) for t in range(2)])
    ]
    own, own_first, own_second = split_rows((near, near_other), ((0,), (1,), (2, 3)))
    own_second = go(own_second, second_flip)
    own_first = go(add(own_first, own_second), first_flip)
    return last_rows([own, own_first, own_second] + far, rows, width)


def solution(mesh):
    placed = (
        P(("groups", "expert"), None),
        P(("groups", "expert"), None),
        P(("groups", "expert"), None),
        P("expert", None, None),
        P("expert", None, None),
        P("expert", None, None),
    )
    return jax.shard_map(
        per_device,
        mesh=mesh,
        in_specs=placed,
        out_specs=P(("groups", "expert"), None),
        check_vma=False,
    )
```
